32 devices in a mesh: gx: 4 (over x, core), gy: 8 (over z, y).
Axes of the slice: x: 2, y: 2, z: 4, core: 2. Of those that a mesh axis runs over, the one named last changes fastest.
Arguments:
- cell_power: float32 [6144, 2048], P(('gx', 'gy')), may hold values from 0.5 to 20
- cell_bin: int32 [6144, 2048], P(('gx', 'gy')), may hold values from 0 to 2047
- block_owner: int32 [6144, 1], P(('gx', 'gy')), may hold values from 0 to 31; in each aligned block of 192 rows (0 to 191, 192 to 383, ...) at most 9 rows name the same one
- block_tile: int32 [6144], P(('gx', 'gy')), may hold values from 0 to 7
- temp_prev: float32 [8, 512, 1024], P(None, 'gx', 'gy'), may hold values from -6 to 6
- cond_x: float32 [8, 512, 1024], P(None, 'gx', 'gy'), may hold values from 0.5 to 4
- cond_y: float32 [8, 512, 1024], P(None, 'gx', 'gy'), may hold values from 0.5 to 4
- cond_z: float32 [8, 512, 1024], P(None, 'gx', 'gy'), may hold values from 1 to 8
- weight: float32 [8, 512, 1024], P(None, 'gx', 'gy'), may hold values from 0.2 to 2
Outputs:
- temperature: float32 [8, 512, 1024], P(None, 'gx', 'gy')
- cell_grad: float32 [2, 6144, 2048], P(None, ('gx', 'gy'))
The draws below stay inside these ranges and needn't reach their ends.
Inputs may be any that keep to these rules, and one draw needn't show every extreme that they name: `block_owner`: among the blocks of one device, at most 9 name the same owner, a bound that some of them reach. `cell_bin`: A bin is the row within the tile times 128 plus the column.
All inputs are finite; a program needn't handle non-finite values.
Results may differ from the reference program's by a relative error of at most 0.00012.
Values sent between devices are 32-bit elements; how exact they have to be, the bound alone decides.
A program may use at most 128 MiB of HBM per device.

```python
import math
import jax
import jax.numpy as jnp
import numpy as np

TX = 128
TY = 128
LZ = 8
TROWS = 16
NBLK = 192
BLK = 2048
MOST = 9
NX = 512
NY = 1024
BLOCKS = 6144
TILES_DEV = 8
BINS = 2048
N_GY = 8
DEVICES = 32


def touch_ends(entries, key, smallest, largest):
    spot = [jax.random.randint(jax.random.fold_in(key, axis), (), 0, length) for axis, length in enumerate(entries.shape)]
    main_axis = entries.shape.index(max(entries.shape))
    next_to = spot[:main_axis] + [(spot[main_axis] + 1) % entries.shape[main_axis]] + spot[main_axis + 1:]
    return entries.at[tuple(spot)].set(smallest).at[tuple(next_to)].set(largest)


def steps_of(stream_key, shape, cuts, smallest, largest):
    gain, own = 1.0, jax.random.fold_in(stream_key, 6)
    for position, blocks in cuts:
        steps = jnp.exp(jax.random.uniform(jax.random.fold_in(own, position), (blocks,), jnp.float32, smallest / len(cuts), largest / len(cuts)))
        gain = gain * jnp.repeat(steps, shape[position] // blocks).reshape([-1 if axis == position else 1 for axis in range(len(shape))])
    return gain


def shared_out(key, own, number, rows, number_of, top, reach, slope):
    ranking = jax.random.permutation(key, number_of)
    crowded, usual = shares(number_of, rows * top, reach, slope, True), shares(number_of, rows * top, reach, slope, False)
    places = jnp.arange(number_of)

    def named(lengths, offset_by):
        used = int((lengths > 0).sum())
        fixed = max(1, used // 4)
        shifted = fixed + (places - fixed + offset_by * (used - fixed)) % max(1, number_of - fixed)
        return jnp.zeros((number_of,), jnp.int32).at[ranking[jnp.where(places < fixed, places, shifted)]].set(jnp.asarray(lengths, jnp.int32))

    lengths = jnp.where(number % 4 == 0, named(crowded, number // 4), named(usual, number - number // 4 - 1))
    mixed = jax.random.permutation(jax.random.fold_in(own, 3), number_of)
    source_of, receiver = mixed[0:number_of // 2 * 2:2], mixed[1:number_of // 2 * 2:2]
    slack = jnp.minimum(lengths[source_of] - 1, reach - lengths[receiver]) // 2
    slack = jnp.where((source_of == ranking[0]) | (receiver == ranking[0]) | (lengths[receiver] == 0), 0, jnp.maximum(slack, 0))
    shifted = jax.random.randint(jax.random.fold_in(own, 4), (number_of // 2,), 0, 1 << 20) % (slack + 1)
    lengths = lengths.at[source_of].add(-shifted).at[receiver].add(shifted)
    items = jnp.searchsorted(jnp.cumsum(lengths), jnp.arange(rows * top), side="right").astype(jnp.int32)
    listing = items.reshape(top, rows).T
    listing = listing[jax.random.permutation(jax.random.fold_in(own, 1), rows)]
    offset_by = jax.random.randint(jax.random.fold_in(own, 2), (rows, 1), 0, top)
    return jnp.take_along_axis(listing, (jnp.arange(top)[None, :] + offset_by) % top, axis=1)


def shares(number_of, total, most, lean, full):
    weights = [(1 << 20) // math.isqrt(grade ** lean) + 1 for grade in range(1, number_of + 1)]
    largest = most if full else min(most, max(-(-total // number_of), total * weights[0] // sum(weights)))
    least = 1 if total - largest >= number_of - 1 else 0
    holding, spare = [largest] + [least] * (number_of - 1), total - largest - least * (number_of - 1)
    while spare > 0:
        free = [i for i in range(1, number_of) if holding[i] < largest] or [i for i in range(1, number_of) if holding[i] < most]
        pool, remaining = sum([weights[i] for i in free]), spare
        for i in free:
            addition = min(most - holding[i], max(1, remaining * weights[i] // pool), spare)
            holding[i] = holding[i] + addition
            spare = spare - addition
    return np.array(holding)


def centred(stream_key, extent, deviation, most, split=(), dtype=jnp.bfloat16):
    entries = jax.random.normal(stream_key, extent, jnp.float32) * deviation
    if len(split) > 0:
        entries = steps_of(stream_key, extent, split, -0.22, 0.18) * entries
    return jnp.clip(entries, min=-most, max=most).astype(dtype)


def setup_inputs(seed: int = 0) -> dict:
    splits = jax.random.split(jax.random.key(seed), 10)
    cell_power = jnp.clip(jnp.exp(math.log(20.0) - 3.6888795 * jax.random.uniform(splits[0], (BLOCKS, BLK), jnp.float32) ** steps_of(splits[0], (BLOCKS, BLK), ((0, 32),), -0.2, 0.2)), 0.5, 20.0)
    cell_bin = touch_ends(jax.random.randint(splits[1], (BLOCKS, BLK), 0, BINS), jax.random.fold_in(splits[1], 1), 0, BINS - 1).astype(jnp.int32)
    block_owner_keys = jax.random.split(jax.random.fold_in(splits[2], 1), BLOCKS // NBLK)
    block_owner_turns = jax.random.permutation(jax.random.fold_in(splits[2], 3), BLOCKS // NBLK)
    block_owner = jax.vmap(lambda own, number: shared_out(jax.random.fold_in(splits[2], 2), own, number, NBLK, DEVICES, 1, MOST, 2))(block_owner_keys, block_owner_turns).reshape((BLOCKS, 1))
    block_tile = touch_ends(jax.random.randint(splits[3], (BLOCKS,), 0, TILES_DEV), jax.random.fold_in(splits[3], 1), 0, TILES_DEV - 1).astype(jnp.int32)
    temp_prev = centred(splits[4], (LZ, NX, NY), 1.0, 6.0, ((1, 4), (2, 8)), jnp.float32)
    cond_x = jnp.clip(jnp.exp(math.log(4.0) - 2.0794415 * jax.random.uniform(splits[5], (LZ, NX, NY), jnp.float32) ** steps_of(splits[5], (LZ, NX, NY), ((1, 4), (2, 8)), -0.2, 0.2)), 0.5, 4.0)
    cond_y = jnp.clip(jnp.exp(math.log(4.0) - 2.0794415 * jax.random.uniform(splits[6], (LZ, NX, NY), jnp.float32) ** steps_of(splits[6], (LZ, NX, NY), ((1, 4), (2, 8)), -0.2, 0.2)), 0.5, 4.0)
    cond_z = jnp.clip(jnp.exp(math.log(8.0) - 2.0794415 * jax.random.uniform(splits[7], (LZ, NX, NY), jnp.float32) ** steps_of(splits[7], (LZ, NX, NY), ((1, 4), (2, 8)), -0.2, 0.2)), 1.0, 8.0)
    weight = jnp.clip(jnp.exp(math.log(2.0) - 2.3025851 * jax.random.uniform(splits[8], (LZ, NX, NY), jnp.float32) ** steps_of(splits[8], (LZ, NX, NY), ((1, 4), (2, 8)), -0.2, 0.2)), 0.2, 2.0)
    return {"cell_power": cell_power, "cell_bin": cell_bin, "block_owner": block_owner, "block_tile": block_tile, "temp_prev": temp_prev, "cond_x": cond_x, "cond_y": cond_y, "cond_z": cond_z, "weight": weight}


def neighbours(field, faces):
    east, west, north, south, upward, downward = faces
    padded = jnp.pad(field, ((0, 0), (1, 1), (1, 1)))
    above = jnp.concatenate([field[1:], jnp.zeros_like(field[:1])], axis=0)
    below = jnp.concatenate([jnp.zeros_like(field[:1]), field[:-1]], axis=0)
    return (east * padded[:, 2:, 1:-1] + west * padded[:, :-2, 1:-1] + north * padded[:, 1:-1, 2:]
            + south * padded[:, 1:-1, :-2] + upward * above + downward * below)


def reference(cell_power, cell_bin, block_owner, block_tile, temp_prev, cond_x, cond_y, cond_z, weight):
    owner = block_owner[:, 0]
    row_start = (owner // N_GY) * TX + block_tile * TROWS
    col_start = (owner % N_GY) * TY
    grid_rows = (row_start[:, None] + cell_bin // TY).astype(jnp.int32)
    grid_cols = (col_start[:, None] + cell_bin % TY).astype(jnp.int32)
    power_map = jnp.zeros((NX, NY), jnp.float32).at[grid_rows, grid_cols].add(cell_power)
    west = jnp.concatenate([jnp.zeros_like(cond_x[:, :1]), cond_x[:, :-1]], axis=1)
    south = jnp.concatenate([jnp.zeros_like(cond_y[:, :, :1]), cond_y[:, :, :-1]], axis=2)
    downward = jnp.concatenate([jnp.zeros_like(cond_z[:1]), cond_z[:-1]], axis=0)
    faces = (cond_x, west, cond_y, south, cond_z, downward)
    diag = cond_x + west + cond_y + south + cond_z + downward
    sweep = temp_prev
    for turn in range(3):
        summed = neighbours(sweep, faces)
        summed = summed.at[0].add(power_map)
        sweep = summed / diag
    adjoint = weight * sweep / diag
    total = adjoint
    for turn in range(2):
        adjoint = neighbours(adjoint, faces) / diag
        total = total + adjoint
    padded = jnp.pad(total[0], 1)
    slope_x = 0.5 * (padded[2:, 1:-1] - padded[:-2, 1:-1])
    slope_y = 0.5 * (padded[1:-1, 2:] - padded[1:-1, :-2])
    grad_x = cell_power * slope_x[grid_rows, grid_cols]
    grad_y = cell_power * slope_y[grid_rows, grid_cols]
    return sweep, jnp.stack([grad_x, grad_y], axis=0)
```

```python
import functools

import jax
import jax.numpy as jnp
from jax import lax
from jax.experimental import pallas as pl
from jax.experimental.pallas import tpu as pltpu
from jax.sharding import PartitionSpec as P

TROWS = 16
GROUP = 8
HALO = 5
PAD_ROWS = 16
VMEM_LIMIT = 48 * 1024 * 1024


def bin_kernel(dest_ref, power_ref, bin_ref, map_ref):
    step = pl.program_id(0)
    cells = power_ref.shape[1]
    cols = map_ref.shape[1]

    @pl.when(step == 0)
    def _():
        map_ref[...] = jnp.zeros_like(map_ref)

    power = power_ref[...]
    bins = bin_ref[...]
    high = power.astype(jnp.bfloat16).astype(jnp.float32)
    low = power - high
    col = lax.bitwise_and(bins, cols - 1)
    row = lax.shift_right_logical(bins, cols.bit_length() - 1)
    col = col.astype(jnp.float32)
    row = row.astype(jnp.float32)
    col_iota = lax.broadcasted_iota(jnp.int32, (cols, cells), 0).astype(jnp.float32).astype(jnp.bfloat16)
    row_iota = lax.broadcasted_iota(jnp.int32, (TROWS, cells), 0).astype(jnp.float32).astype(jnp.bfloat16)
    one = jnp.ones((), jnp.bfloat16)
    zero = jnp.zeros((), jnp.bfloat16)
    for s in range(GROUP):
        def spread(x, n):
            return jnp.broadcast_to(x[s : s + 1, :], (n, cells)).astype(jnp.bfloat16)

        col_hot = jnp.where(spread(col, cols) == col_iota, one, zero)
        row_mask = spread(row, TROWS) == row_iota
        left = jnp.concatenate(
            [
                jnp.where(row_mask, spread(high, TROWS), zero),
                jnp.where(row_mask, spread(low, TROWS), zero),
            ],
            axis=0,
        )
        tile = lax.dot_general(
            left, col_hot, (((1,), (1,)), ((), ())), preferred_element_type=jnp.float32
        )
        start = pl.multiple_of(dest_ref[step * GROUP + s] * TROWS, TROWS)
        map_ref[pl.ds(start, TROWS), :] += tile[:TROWS] + tile[TROWS:]


def bin_cells(dest, cell_power, cell_bin, map_rows, cols):
    blocks, cells = cell_power.shape
    return pl.pallas_call(
        bin_kernel,
        grid_spec=pltpu.PrefetchScalarGridSpec(
            num_scalar_prefetch=1,
            grid=(blocks // GROUP,),
            in_specs=[pl.BlockSpec((GROUP, cells), lambda i, d: (i, 0))] * 2,
            out_specs=pl.BlockSpec((map_rows, cols), lambda i, d: (0, 0)),
        ),
        out_shape=jax.ShapeDtypeStruct((map_rows, cols), jnp.float32),
        compiler_params=pltpu.CompilerParams(vmem_limit_bytes=VMEM_LIMIT),
        cost_estimate=pl.CostEstimate(
            flops=blocks * cells * cols * TROWS * 12, bytes_accessed=40 * 1024 * 1024, transcendentals=0
        ),
        name="bin_cells",
    )(dest, cell_power, cell_bin)


def grad_kernel(size_gx, size_gy, dest_ref, power_ref, bin_ref, sens_ref, out_ref, slope_ref, table_ref):
    step = pl.program_id(0)
    cells = power_ref.shape[1]
    owners, rows, cols = sens_ref.shape

    @pl.when(step == 0)
    def _():
        row_id = lax.broadcasted_iota(jnp.int32, (rows, cols), 0)
        col_id = lax.broadcasted_iota(jnp.int32, (rows, cols), 1)

        def one(o, carry):
            i = o // size_gy
            j = lax.rem(o, size_gy)
            here = sens_ref[o]
            above = sens_ref[jnp.maximum(o - size_gy, 0), rows - 1 :, :]
            below = sens_ref[jnp.minimum(o + size_gy, owners - 1), :1, :]
            above = jnp.where(i > 0, above, 0.0)
            below = jnp.where(i < size_gx - 1, below, 0.0)
            before = pltpu.roll(sens_ref[jnp.maximum(o - 1, 0)], 1, 1)
            after = pltpu.roll(sens_ref[jnp.minimum(o + 1, owners - 1)], cols - 1, 1)
            before = jnp.where(j > 0, before, 0.0)
            after = jnp.where(j < size_gy - 1, after, 0.0)
            down = jnp.where(row_id == rows - 1, below, pltpu.roll(here, rows - 1, 0))
            up = jnp.where(row_id == 0, above, pltpu.roll(here, 1, 0))
            right = jnp.where(col_id == cols - 1, after, pltpu.roll(here, cols - 1, 1))
            left = jnp.where(col_id == 0, before, pltpu.roll(here, 1, 1))
            at = pl.ds(pl.multiple_of(o * rows, rows), rows)
            slope_ref[0, at, :] = 0.5 * (down - up)
            slope_ref[1, at, :] = 0.5 * (right - left)
            return carry

        lax.fori_loop(0, owners, one, 0)

    for s in range(GROUP):
        start = pl.multiple_of(dest_ref[step * GROUP + s] * TROWS, TROWS)
        for a in range(2):
            table_ref[a, :, s, :] = slope_ref[a, pl.ds(start, TROWS), :]
    for c in range(cells // cols):
        at = slice(c * cols, (c + 1) * cols)
        bins = bin_ref[:, at]
        power = power_ref[:, at]
        col = lax.bitwise_and(bins, cols - 1)
        row = lax.shift_right_logical(bins, cols.bit_length() - 1)
        masks = [lax.bitwise_and(row, 1 << b) != 0 for b in range(4)]
        for a in range(2):
            picks = [
                jnp.take_along_axis(table_ref[a, r], col, axis=1, mode="promise_in_bounds")
                for r in range(TROWS)
            ]
            for mask in masks:
                picks = [jnp.where(mask, picks[2 * k + 1], picks[2 * k]) for k in range(len(picks) // 2)]
            out_ref[a, :, at] = picks[0] * power


def cell_grads(dest, cell_power, cell_bin, sens, size_gx, size_gy):
    blocks, cells = cell_power.shape
    owners, rows, cols = sens.shape
    return pl.pallas_call(
        functools.partial(grad_kernel, size_gx, size_gy),
        grid_spec=pltpu.PrefetchScalarGridSpec(
            num_scalar_prefetch=1,
            grid=(blocks // GROUP,),
            in_specs=[pl.BlockSpec((GROUP, cells), lambda i, d: (i, 0))] * 2
            + [pl.BlockSpec((owners, rows, cols), lambda i, d: (0, 0, 0))],
            out_specs=pl.BlockSpec((2, GROUP, cells), lambda i, d: (0, i, 0)),
            scratch_shapes=[
                pltpu.VMEM((2, owners * rows, cols), jnp.float32),
                pltpu.VMEM((2, TROWS, GROUP, cols), jnp.float32),
            ],
        ),
        out_shape=jax.ShapeDtypeStruct((2, blocks, cells), jnp.float32),
        compiler_params=pltpu.CompilerParams(vmem_limit_bytes=VMEM_LIMIT),
        name="cell_grads",
    )(dest, cell_power, cell_bin, sens)


def roll(x, distance, axis):
    return pltpu.roll(x, distance % x.shape[axis], axis)


def sweep_kernel(mask_ref, stack_ref, power_ref, temp_out, sens_out, west_s, south_s, inv_s, a_s, b_s):
    layers = stack_ref.shape[1]
    mask = mask_ref[...]
    for l in range(layers):
        east = stack_ref[1, l]
        north = stack_ref[2, l]
        west = roll(east, 1, 0)
        south = roll(north, 1, 1)
        diag = east + west + north + south + stack_ref[3, l]
        if l:
            diag = diag + stack_ref[3, l - 1]
        west_s[l] = west
        south_s[l] = south
        inv_s[l] = jnp.where(mask > 0.0, 1.0 / diag, 0.0)

    def coupling(field, l):
        v = field(l)
        out = (
            stack_ref[1, l] * roll(v, -1, 0)
            + west_s[l] * roll(v, 1, 0)
            + stack_ref[2, l] * roll(v, -1, 1)
            + south_s[l] * roll(v, 1, 1)
        )
        if l + 1 < layers:
            out = out + stack_ref[3, l] * field(l + 1)
        if l:
            out = out + stack_ref[3, l - 1] * field(l - 1)
        return out

    def sweep(field, out_ref):
        for l in range(layers):
            summed = coupling(field, l)
            if l == 0:
                summed = summed + power_ref[...]
            out_ref[l] = summed * inv_s[l]

    rows, cols = sens_out.shape
    sweep(lambda l: stack_ref[0, l], a_s)
    sweep(lambda l: a_s[l], b_s)
    sweep(lambda l: b_s[l], a_s)
    for l in range(layers):
        temp_out[l] = a_s[l, :rows, :cols]
        b_s[l] = stack_ref[4, l] * a_s[l] * inv_s[l]
    for l in range(2):
        a_s[l] = coupling(lambda k: b_s[k], l) * inv_s[l]
    last = coupling(lambda k: a_s[k], 0) * inv_s[0]
    total = b_s[0] + a_s[0] + last
    sens_out[...] = total[:rows, :cols]


def sweeps(mask, stack, power, rows, cols):
    _, layers, wide_rows, wide_cols = stack.shape
    field = pltpu.VMEM((layers, wide_rows, wide_cols), jnp.float32)
    return pl.pallas_call(
        sweep_kernel,
        out_shape=(
            jax.ShapeDtypeStruct((layers, rows, cols), jnp.float32),
            jax.ShapeDtypeStruct((rows, cols), jnp.float32),
        ),
        in_specs=[pl.BlockSpec(memory_space=pltpu.VMEM)] * 3,
        out_specs=(pl.BlockSpec(memory_space=pltpu.VMEM),) * 2,
        scratch_shapes=[field] * 5,
        compiler_params=pltpu.CompilerParams(vmem_limit_bytes=VMEM_LIMIT),
        name="sweeps",
    )(mask, stack, power)


def padded(array, width, row_dim):
    for axis, dim, room in (("gx", row_dim, PAD_ROWS), ("gy", row_dim + 1, array.shape[row_dim + 1])):
        peers = lax.axis_size(axis)
        length = array.shape[dim] if dim == row_dim else room
        up = [(i, i + 1) for i in range(peers - 1)]
        down = [(j, i) for i, j in up]
        last = lax.slice_in_dim(array, length - width, length, axis=dim)
        first = lax.slice_in_dim(array, 0, width, axis=dim)
        before = lax.ppermute(last, axis, up)
        after = lax.ppermute(first, axis, down)
        shape = list(array.shape)
        shape[dim] = room - 2 * width
        gap = jnp.zeros(shape, array.dtype)
        array = jnp.concatenate([array, after, gap, before], axis=dim)
    return array


def inside_mask(rows, cols):
    def axis_ok(axis, length, room):
        place = lax.broadcasted_iota(jnp.int32, (length + room,), 0)
        offset = jnp.where(place >= length + room // 2, place - (length + room), place)
        near = (offset >= -(HALO - 1)) & (offset < length + HALO - 1)
        whole = lax.axis_index(axis) * length + offset
        return near & (whole >= 0) & (whole < length * lax.axis_size(axis))

    ok = axis_ok("gx", rows, PAD_ROWS)[:, None] & axis_ok("gy", cols, cols)[None, :]
    return ok.astype(jnp.float32)


def on_device(
    cell_power, cell_bin, block_owner, block_tile, temp_prev, cond_x, cond_y, cond_z, weight
):
    _, rows, cols = temp_prev.shape
    tiles = rows // TROWS
    size_gx, size_gy = lax.axis_size("gx"), lax.axis_size("gy")
    devices = size_gx * size_gy
    dest = block_owner[:, 0] * tiles + block_tile
    stack = padded(jnp.stack([temp_prev, cond_x, cond_y, cond_z, weight]), HALO, 2)
    mask = inside_mask(rows, cols)
    partial = bin_cells(dest, cell_power, cell_bin, devices * rows, cols)
    power_map = lax.psum_scatter(partial, ("gx", "gy"), scatter_dimension=0, tiled=True)
    power_map = padded(power_map, HALO - 1, 0)
    temperature, sensitivity = sweeps(mask, stack, power_map, rows, cols)
    sens = lax.all_gather(sensitivity, ("gx", "gy"), axis=0, tiled=False)
    grads = cell_grads(dest, cell_power, cell_bin, sens, size_gx, size_gy)
    return temperature, grads


def solution(mesh):
    cells = P(("gx", "gy"), None)
    grid = P(None, "gx", "gy")
    return jax.shard_map(
        on_device,
        mesh=mesh,
        in_specs=(cells, cells, cells, P(("gx", "gy")), grid, grid, grid, grid, grid),
        out_specs=(grid, P(None, ("gx", "gy"), None)),
        check_vma=False,
    )
```

```python
import functools

import jax
import jax.numpy as jnp
from jax import lax
from jax.experimental import pallas as pl
from jax.experimental.pallas import tpu as pltpu
from jax.sharding import PartitionSpec as P

TROWS = 16
GROUP = 8
HALO = 5
PAD_ROWS = 16
VMEM_LIMIT = 48 * 1024 * 1024


def bin_kernel(dest_ref, power_ref, bin_ref, map_ref):
    step = pl.program_id(0)
    cells = power_ref.shape[1]
    cols = map_ref.shape[1]

    @pl.when(step == 0)
    def _():
        map_ref[...] = jnp.zeros_like(map_ref)

    power = power_ref[...]
    bins = bin_ref[...]
    high = power.astype(jnp.bfloat16).astype(jnp.float32)
    low = power - high
    col = lax.bitwise_and(bins, cols - 1)
    row = lax.shift_right_logical(bins, cols.bit_length() - 1)
    col = col.astype(jnp.float32)
    row = row.astype(jnp.float32)
    col_iota = lax.broadcasted_iota(jnp.int32, (cols, cells), 0).astype(jnp.float32).astype(jnp.bfloat16)
    row_iota = lax.broadcasted_iota(jnp.int32, (TROWS, cells), 0).astype(jnp.float32).astype(jnp.bfloat16)
    one = jnp.ones((), jnp.bfloat16)
    zero = jnp.zeros((), jnp.bfloat16)
    for s in range(GROUP):
        def spread(x, n):
            return jnp.broadcast_to(x[s : s + 1, :], (n, cells)).astype(jnp.bfloat16)

        col_hot = jnp.where(spread(col, cols) == col_iota, one, zero)
        row_mask = spread(row, TROWS) == row_iota
        left = jnp.concatenate(
            [
                jnp.where(row_mask, spread(high, TROWS), zero),
                jnp.where(row_mask, spread(low, TROWS), zero),
            ],
            axis=0,
        )
        tile = lax.dot_general(
            left, col_hot, (((1,), (1,)), ((), ())), preferred_element_type=jnp.float32
        )
        start = pl.multiple_of(dest_ref[step * GROUP + s] * TROWS, TROWS)
        map_ref[pl.ds(start, TROWS), :] += tile[:TROWS] + tile[TROWS:]


def bin_cells(dest, cell_power, cell_bin, map_rows, cols):
    blocks, cells = cell_power.shape
    return pl.pallas_call(
        bin_kernel,
        grid_spec=pltpu.PrefetchScalarGridSpec(
            num_scalar_prefetch=1,
            grid=(blocks // GROUP,),
            in_specs=[pl.BlockSpec((GROUP, cells), lambda i, d: (i, 0))] * 2,
            out_specs=pl.BlockSpec((map_rows, cols), lambda i, d: (0, 0)),
        ),
        out_shape=jax.ShapeDtypeStruct((map_rows, cols), jnp.float32),
        compiler_params=pltpu.CompilerParams(vmem_limit_bytes=VMEM_LIMIT),
        cost_estimate=pl.CostEstimate(
            flops=blocks * cells * cols * TROWS * 12, bytes_accessed=40 * 1024 * 1024, transcendentals=0
        ),
        name="bin_cells",
    )(dest, cell_power, cell_bin)


def grad_kernel(size_gx, size_gy, dest_ref, power_ref, bin_ref, sens_ref, out_ref, slope_ref, table_ref):
    step = pl.program_id(0)
    cells = power_ref.shape[1]
    owners, rows, cols = sens_ref.shape

    @pl.when(step == 0)
    def _():
        row_id = lax.broadcasted_iota(jnp.int32, (rows, cols), 0)
        col_id = lax.broadcasted_iota(jnp.int32, (rows, cols), 1)

        def one(o, carry):
            i = o // size_gy
            j = lax.rem(o, size_gy)
            here = sens_ref[o]
            above = sens_ref[jnp.maximum(o - size_gy, 0), rows - 1 :, :]
            below = sens_ref[jnp.minimum(o + size_gy, owners - 1), :1, :]
            above = jnp.where(i > 0, above, 0.0)
            below = jnp.where(i < size_gx - 1, below, 0.0)
            before = pltpu.roll(sens_ref[jnp.maximum(o - 1, 0)], 1, 1)
            after = pltpu.roll(sens_ref[jnp.minimum(o + 1, owners - 1)], cols - 1, 1)
            before = jnp.where(j > 0, before, 0.0)
            after = jnp.where(j < size_gy - 1, after, 0.0)
            down = jnp.where(row_id == rows - 1, below, pltpu.roll(here, rows - 1, 0))
            up = jnp.where(row_id == 0, above, pltpu.roll(here, 1, 0))
            right = jnp.where(col_id == cols - 1, after, pltpu.roll(here, cols - 1, 1))
            left = jnp.where(col_id == 0, before, pltpu.roll(here, 1, 1))
            at = pl.ds(pl.multiple_of(o * rows, rows), rows)
            slope_ref[0, at, :] = 0.5 * (down - up)
            slope_ref[1, at, :] = 0.5 * (right - left)
            return carry

        lax.fori_loop(0, owners, one, 0)

    for s in range(GROUP):
        start = pl.multiple_of(dest_ref[step * GROUP + s] * TROWS, TROWS)
        for a in range(2):
            table_ref[a, :, s, :] = slope_ref[a, pl.ds(start, TROWS), :]
    for c in range(cells // cols):
        at = slice(c * cols, (c + 1) * cols)
        bins = bin_ref[:, at]
        power = power_ref[:, at]
        col = lax.bitwise_and(bins, cols - 1)
        row = lax.shift_right_logical(bins, cols.bit_length() - 1)
        masks = [lax.bitwise_and(row, 1 << b) != 0 for b in range(4)]
        for a in range(2):
            picks = [
                jnp.take_along_axis(table_ref[a, r], col, axis=1, mode="promise_in_bounds")
                for r in range(TROWS)
            ]
            for mask in masks:
                picks = [jnp.where(mask, picks[2 * k + 1], picks[2 * k]) for k in range(len(picks) // 2)]
            out_ref[a, :, at] = picks[0] * power


def cell_grads(dest, cell_power, cell_bin, sens, size_gx, size_gy):
    blocks, cells = cell_power.shape
    owners, rows, cols = sens.shape
    return pl.pallas_call(
        functools.partial(grad_kernel, size_gx, size_gy),
        grid_spec=pltpu.PrefetchScalarGridSpec(
            num_scalar_prefetch=1,
            grid=(blocks // GROUP,),
            in_specs=[pl.BlockSpec((GROUP, cells), lambda i, d: (i, 0))] * 2
            + [pl.BlockSpec((owners, rows, cols), lambda i, d: (0, 0, 0))],
            out_specs=pl.BlockSpec((2, GROUP, cells), lambda i, d: (0, i, 0)),
            scratch_shapes=[
                pltpu.VMEM((2, owners * rows, cols), jnp.float32),
                pltpu.VMEM((2, TROWS, GROUP, cols), jnp.float32),
            ],
        ),
        out_shape=jax.ShapeDtypeStruct((2, blocks, cells), jnp.float32),
        compiler_params=pltpu.CompilerParams(vmem_limit_bytes=VMEM_LIMIT),
        name="cell_grads",
    )(dest, cell_power, cell_bin, sens)


def roll(x, distance, axis):
    return pltpu.roll(x, distance % x.shape[axis], axis)


def remote(src, dst, sems, at, device):
    return pltpu.make_async_remote_copy(
        src_ref=src,
        dst_ref=dst,
        send_sem=sems.at[(0, *at)],
        recv_sem=sems.at[(1, *at)],
        device_id=device,
        device_id_type=pl.DeviceIdType.MESH,
    )


def sweep_kernel(
    size_gx,
    size_gy,
    mask_ref,
    stack_ref,
    partial_ref,
    temp_out,
    sens_out,
    west_s,
    south_s,
    inv_s,
    a_s,
    b_s,
    core_buf,
    x_buf,
    x_sum,
    y_buf,
    wide,
    sides,
    power_s,
    sens,
    core_sems,
    x_sems,
    y_sems,
    halo_sems,
    back_y,
    back_x,
    back_core,
):
    layers = stack_ref.shape[1]
    _, rows, cols = partial_ref.shape
    size_x = size_gx // 2
    gx, gy = lax.axis_index("gx"), lax.axis_index("gy")
    x, core = gx // 2, lax.rem(gx, 2)
    partner = (x * 2 + 1 - core, gy)

    def ahead(dj):
        return lax.rem(gy + dj, size_gy)

    def behind(dj):
        return lax.rem(gy + size_gy - dj, size_gy)

    def x_ahead(d):
        return lax.rem(x + d, size_x)

    def x_behind(d):
        return lax.rem(x + size_x - d, size_x)

    barrier = pltpu.get_barrier_semaphore()
    for d in range(1, size_gx):
        pl.semaphore_signal(
            barrier,
            inc=1,
            device_id=(lax.rem(gx + d, size_gx), gy),
            device_id_type=pl.DeviceIdType.MESH,
        )
    for d in range(1, size_gy):
        pl.semaphore_signal(
            barrier, inc=1, device_id=(gx, ahead(d)), device_id_type=pl.DeviceIdType.MESH
        )
    pl.semaphore_wait(barrier, size_gx + size_gy - 2)

    def to_core(dj, t):
        src = partial_ref.at[(t * 2 + 1 - core) * size_gy + ahead(dj)]
        return remote(src, core_buf.at[t, dj], core_sems, (t, dj), partner)

    def to_x(dj, d):
        src = core_buf.at[x_ahead(d), dj]
        return remote(src, x_buf.at[d - 1, dj], x_sems, (d - 1, dj), (x_ahead(d) * 2 + core, gy))

    def to_y(dj):
        return remote(x_sum.at[dj], y_buf.at[dj - 1], y_sems, (dj - 1,), (gx, ahead(dj)))

    def chunk(k):
        return lax.rem(k + 1, size_gy)

    def loop(count, body, start=0):
        def wrapped(k, carry):
            body(k)
            return carry

        lax.fori_loop(start, count, wrapped, 0)

    def send_core(k):
        for t in range(size_x):
            to_core(chunk(k), t).start()

    loop(size_gy, send_core)

    mask = mask_ref[...]
    for l in range(layers):
        east = stack_ref[1, l]
        north = stack_ref[2, l]
        west = roll(east, 1, 0)
        south = roll(north, 1, 1)
        diag = east + west + north + south + stack_ref[3, l]
        if l:
            diag = diag + stack_ref[3, l - 1]
        west_s[l] = west
        south_s[l] = south
        inv_s[l] = jnp.where(mask > 0.0, 1.0 / diag, 0.0)

    def send_x(k):
        dj = chunk(k)
        for t in range(size_x):
            to_core(dj, t).wait_recv()
            core_buf[t, dj] += partial_ref[(t * 2 + core) * size_gy + ahead(dj)]
        for d in range(1, size_x):
            to_x(dj, d).start()

    loop(size_gy, send_x)

    def add_x(dj):
        total = core_buf[x, dj]
        for d in range(1, size_x):
            to_x(dj, d).wait_recv()
            total = total + x_buf[d - 1, dj]
        x_sum[dj] = total

    def send_y(dj):
        add_x(dj)
        to_y(dj).start()

    loop(size_gy, send_y, 1)
    add_x(0)
    wide[:rows] = x_sum[0]

    def add_y(dj):
        to_y(dj).wait_recv()
        wide[:rows] += y_buf[dj - 1]

    loop(size_gy, add_y, 1)

    up, down = lax.rem(gx + 1, size_gx), lax.rem(gx + size_gx - 1, size_gx)
    halo_rows = (
        remote(wide.at[pl.ds(rows - 8, 8)], wide.at[pl.ds(rows + 8, 8)], halo_sems, (0,), (up, gy)),
        remote(wide.at[pl.ds(0, 8)], wide.at[pl.ds(rows, 8)], halo_sems, (1,), (down, gy)),
    )
    for copy in halo_rows:
        copy.start()
    for copy in halo_rows:
        copy.wait()
    halo_cols = (
        remote(wide, sides.at[0], halo_sems, (2,), (gx, ahead(1))),
        remote(wide, sides.at[1], halo_sems, (3,), (gx, behind(1))),
    )
    for copy in halo_cols:
        copy.start()
    for copy in halo_cols:
        copy.wait()
    lane = lax.broadcasted_iota(jnp.int32, wide.shape, 1)
    power_s[:, :cols] = wide[...]
    power_s[:, cols:] = jnp.where(lane < cols // 2, sides[1], sides[0])

    def coupling(field, l):
        v = field(l)
        out = (
            stack_ref[1, l] * roll(v, -1, 0)
            + west_s[l] * roll(v, 1, 0)
            + stack_ref[2, l] * roll(v, -1, 1)
            + south_s[l] * roll(v, 1, 1)
        )
        if l + 1 < layers:
            out = out + stack_ref[3, l] * field(l + 1)
        if l:
            out = out + stack_ref[3, l - 1] * field(l - 1)
        return out

    def sweep(field, out_ref):
        for l in range(layers):
            summed = coupling(field, l)
            if l == 0:
                summed = summed + power_s[...]
            out_ref[l] = summed * inv_s[l]

    sweep(lambda l: stack_ref[0, l], a_s)
    sweep(lambda l: a_s[l], b_s)
    sweep(lambda l: b_s[l], a_s)
    for l in range(layers):
        temp_out[l] = a_s[l, :rows, :cols]
        b_s[l] = stack_ref[4, l] * a_s[l] * inv_s[l]
    for l in range(2):
        a_s[l] = coupling(lambda k: b_s[k], l) * inv_s[l]
    last = coupling(lambda k: a_s[k], 0) * inv_s[0]
    total = b_s[0] + a_s[0] + last
    sens[gx * size_gy + gy] = total[:rows, :cols]

    def give_y(dj):
        mine = sens.at[gx * size_gy + gy]
        return remote(mine, mine, back_y, (dj - 1,), (gx, ahead(dj)))

    def give_x(dj, d):
        block = sens.at[gx * size_gy + behind(dj)]
        return remote(block, block, back_x, (d - 1, dj), (x_ahead(d) * 2 + core, gy))

    def give_core(dj, d):
        block = sens.at[(x_behind(d) * 2 + core) * size_gy + behind(dj)]
        return remote(block, block, back_core, (d, dj), partner)

    def pass_on(dj):
        for d in range(1, size_x):
            give_x(dj, d).start()
        give_core(dj, 0).start()

    def receive_y(dj):
        give_y(dj).wait_recv()
        pass_on(dj)

    def receive_x(dj):
        for d in range(1, size_x):
            give_x(dj, d).wait_recv()
            give_core(dj, d).start()

    def finish(dj):
        for d in range(size_x):
            give_core(dj, d).wait_recv()
            give_core(dj, d).wait_send()
            to_core(dj, d).wait_send()
        for d in range(1, size_x):
            give_x(dj, d).wait_send()
            to_x(dj, d).wait_send()

    def finish_y(dj):
        give_y(dj).wait_send()
        to_y(dj).wait_send()

    loop(size_gy, lambda dj: give_y(dj).start(), 1)
    pass_on(0)
    loop(size_gy, receive_y, 1)
    loop(size_gy, receive_x)
    loop(size_gy, finish)
    loop(size_gy, finish_y, 1)

    def store(o):
        sens_out[o] = sens[o]

    loop(size_gx * size_gy, store)


def sweeps(mask, stack, partial, size_gx, size_gy):
    owners, rows, cols = partial.shape
    _, layers, wide_rows, wide_cols = stack.shape
    size_x = size_gx // 2
    vmem = pl.BlockSpec(memory_space=pltpu.VMEM)

    def blocks(*lead, length=rows):
        return pltpu.VMEM((*lead, length, cols), jnp.float32)

    def sems(*shape):
        return pltpu.SemaphoreType.DMA((2, *shape))

    return pl.pallas_call(
        functools.partial(sweep_kernel, size_gx, size_gy),
        out_shape=(
            jax.ShapeDtypeStruct((layers, rows, cols), jnp.float32),
            jax.ShapeDtypeStruct((owners, rows, cols), jnp.float32),
        ),
        in_specs=[vmem] * 3,
        out_specs=(vmem, vmem),
        scratch_shapes=[pltpu.VMEM((layers, wide_rows, wide_cols), jnp.float32)] * 5
        + [
            blocks(size_x, size_gy),
            blocks(size_x - 1, size_gy),
            blocks(size_gy),
            blocks(size_gy - 1),
            blocks(length=wide_rows),
            blocks(2, length=wide_rows),
            pltpu.VMEM((wide_rows, wide_cols), jnp.float32),
            blocks(owners),
            sems(size_x, size_gy),
            sems(size_x - 1, size_gy),
            sems(size_gy - 1),
            sems(4),
            sems(size_gy - 1),
            sems(size_x - 1, size_gy),
            sems(size_x, size_gy),
        ],
        compiler_params=pltpu.CompilerParams(
            vmem_limit_bytes=56 * 1024 * 1024, collective_id=0, has_side_effects=True
        ),
        name="sweeps",
    )(mask, stack, partial)


def padded(array, width, row_dim):
    for axis, dim, room in (("gx", row_dim, PAD_ROWS), ("gy", row_dim + 1, array.shape[row_dim + 1])):
        peers = lax.axis_size(axis)
        length = array.shape[dim] if dim == row_dim else room
        up = [(i, i + 1) for i in range(peers - 1)]
        down = [(j, i) for i, j in up]
        last = lax.slice_in_dim(array, length - width, length, axis=dim)
        first = lax.slice_in_dim(array, 0, width, axis=dim)
        before = lax.ppermute(last, axis, up)
        after = lax.ppermute(first, axis, down)
        shape = list(array.shape)
        shape[dim] = room - 2 * width
        gap = jnp.zeros(shape, array.dtype)
        array = jnp.concatenate([array, after, gap, before], axis=dim)
    return array


def inside_mask(rows, cols):
    def axis_ok(axis, length, room):
        place = lax.broadcasted_iota(jnp.int32, (length + room,), 0)
        offset = jnp.where(place >= length + room // 2, place - (length + room), place)
        near = (offset >= -(HALO - 1)) & (offset < length + HALO - 1)
        whole = lax.axis_index(axis) * length + offset
        return near & (whole >= 0) & (whole < length * lax.axis_size(axis))

    ok = axis_ok("gx", rows, PAD_ROWS)[:, None] & axis_ok("gy", cols, cols)[None, :]
    return ok.astype(jnp.float32)


def on_device(
    cell_power, cell_bin, block_owner, block_tile, temp_prev, cond_x, cond_y, cond_z, weight
):
    _, rows, cols = temp_prev.shape
    tiles = rows // TROWS
    size_gx, size_gy = lax.axis_size("gx"), lax.axis_size("gy")
    devices = size_gx * size_gy
    dest = block_owner[:, 0] * tiles + block_tile
    stack = padded(jnp.stack([temp_prev, cond_x, cond_y, cond_z, weight]), HALO, 2)
    mask = inside_mask(rows, cols)
    partial = bin_cells(dest, cell_power, cell_bin, devices * rows, cols)
    partial = partial.reshape(devices, rows, cols)
    temperature, sens = sweeps(mask, stack, partial, size_gx, size_gy)
    grads = cell_grads(dest, cell_power, cell_bin, sens, size_gx, size_gy)
    return temperature, grads


def solution(mesh):
    cells = P(("gx", "gy"), None)
    grid = P(None, "gx", "gy")
    return jax.shard_map(
        on_device,
        mesh=mesh,
        in_specs=(cells, cells, cells, P(("gx", "gy")), grid, grid, grid, grid, grid),
        out_specs=(grid, P(None, ("gx", "gy"), None)),
        check_vma=False,
    )
```

```python
import functools

import jax
import jax.numpy as jnp
from jax import lax
from jax.experimental import pallas as pl
from jax.experimental.pallas import tpu as pltpu
from jax.sharding import PartitionSpec as P

TROWS = 16
GROUP = 8
HALO = 5
PAD_ROWS = 16
SLOT = 8
VMEM_LIMIT = 48 * 1024 * 1024


def bin_kernel(dest_ref, power_ref, bin_ref, map_ref):
    step = pl.program_id(0)
    cells = power_ref.shape[1]
    cols = map_ref.shape[1]

    @pl.when(step == 0)
    def _():
        map_ref[...] = jnp.zeros_like(map_ref)

    power = power_ref[...]
    bins = bin_ref[...]
    high = power.astype(jnp.bfloat16)
    low = (power - high.astype(jnp.float32)).astype(jnp.bfloat16)
    col = lax.bitwise_and(bins, cols - 1)
    row = lax.shift_right_logical(bins, cols.bit_length() - 1)
    col = col.astype(jnp.float32).astype(jnp.bfloat16)
    row = row.astype(jnp.float32).astype(jnp.bfloat16)
    col_iota = lax.broadcasted_iota(jnp.int32, (cols, cells), 0).astype(jnp.float32).astype(jnp.bfloat16)
    row_iota = lax.broadcasted_iota(jnp.int32, (TROWS, cells), 0).astype(jnp.float32).astype(jnp.bfloat16)
    one = jnp.ones((), jnp.bfloat16)
    zero = jnp.zeros((), jnp.bfloat16)
    for s in range(GROUP):
        def spread(x, n):
            return jnp.broadcast_to(x[s : s + 1, :], (n, cells))

        col_hot = jnp.where(spread(col, cols) == col_iota, one, zero)
        row_mask = spread(row, TROWS) == row_iota
        left = jnp.concatenate(
            [
                jnp.where(row_mask, spread(high, TROWS), zero),
                jnp.where(row_mask, spread(low, TROWS), zero),
            ],
            axis=0,
        )
        tile = lax.dot_general(
            left, col_hot, (((1,), (1,)), ((), ())), preferred_element_type=jnp.float32
        )
        start = pl.multiple_of(dest_ref[step * GROUP + s] * TROWS, TROWS)
        map_ref[pl.ds(start, TROWS), :] += tile[:TROWS] + tile[TROWS:]


def bin_cells(dest, cell_power, cell_bin, map_rows, cols):
    blocks, cells = cell_power.shape
    return pl.pallas_call(
        bin_kernel,
        grid_spec=pltpu.PrefetchScalarGridSpec(
            num_scalar_prefetch=1,
            grid=(blocks // GROUP,),
            in_specs=[pl.BlockSpec((GROUP, cells), lambda i, d: (i, 0))] * 2,
            out_specs=pl.BlockSpec((map_rows, cols), lambda i, d: (0, 0)),
        ),
        out_shape=jax.ShapeDtypeStruct((map_rows, cols), jnp.float32),
        compiler_params=pltpu.CompilerParams(vmem_limit_bytes=VMEM_LIMIT),
        cost_estimate=pl.CostEstimate(
            flops=blocks * cells * cols * TROWS * 12, bytes_accessed=40 * 1024 * 1024, transcendentals=0
        ),
        name="bin_cells",
    )(dest, cell_power, cell_bin)


def grad_kernel(size_gx, size_gy, dest_ref, power_ref, bin_ref, sens_ref, out_ref, slope_ref, table_ref):
    step = pl.program_id(0)
    cells = power_ref.shape[1]
    owners, rows, cols = sens_ref.shape

    @pl.when(step == 0)
    def _():
        row_id = lax.broadcasted_iota(jnp.int32, (rows, cols), 0)
        col_id = lax.broadcasted_iota(jnp.int32, (rows, cols), 1)

        def one(o, carry):
            i = o // size_gy
            j = lax.rem(o, size_gy)
            here = sens_ref[o]
            above = sens_ref[jnp.maximum(o - size_gy, 0), rows - 1 :, :]
            below = sens_ref[jnp.minimum(o + size_gy, owners - 1), :1, :]
            above = jnp.where(i > 0, above, 0.0)
            below = jnp.where(i < size_gx - 1, below, 0.0)
            before = pltpu.roll(sens_ref[jnp.maximum(o - 1, 0)], 1, 1)
            after = pltpu.roll(sens_ref[jnp.minimum(o + 1, owners - 1)], cols - 1, 1)
            before = jnp.where(j > 0, before, 0.0)
            after = jnp.where(j < size_gy - 1, after, 0.0)
            down = jnp.where(row_id == rows - 1, below, pltpu.roll(here, rows - 1, 0))
            up = jnp.where(row_id == 0, above, pltpu.roll(here, 1, 0))
            right = jnp.where(col_id == cols - 1, after, pltpu.roll(here, cols - 1, 1))
            left = jnp.where(col_id == 0, before, pltpu.roll(here, 1, 1))
            at = pl.ds(pl.multiple_of(o * rows, rows), rows)
            slope_ref[0, at, :] = 0.5 * (down - up)
            slope_ref[1, at, :] = 0.5 * (right - left)
            return carry

        lax.fori_loop(0, owners, one, 0)

    for s in range(GROUP):
        start = pl.multiple_of(dest_ref[step * GROUP + s] * TROWS, TROWS)
        for a in range(2):
            table_ref[a, :, s, :] = slope_ref[a, pl.ds(start, TROWS), :]
    for c in range(cells // cols):
        at = slice(c * cols, (c + 1) * cols)
        bins = bin_ref[:, at]
        power = power_ref[:, at]
        col = lax.bitwise_and(bins, cols - 1)
        row = lax.shift_right_logical(bins, cols.bit_length() - 1)
        masks = [lax.bitwise_and(row, 1 << b) != 0 for b in range(4)]
        for a in range(2):
            picks = [
                jnp.take_along_axis(table_ref[a, r], col, axis=1, mode="promise_in_bounds")
                for r in range(TROWS)
            ]
            for mask in masks:
                picks = [jnp.where(mask, picks[2 * k + 1], picks[2 * k]) for k in range(len(picks) // 2)]
            out_ref[a, :, at] = picks[0] * power


def cell_grads(dest, cell_power, cell_bin, sens, size_gx, size_gy):
    blocks, cells = cell_power.shape
    owners, rows, cols = sens.shape
    return pl.pallas_call(
        functools.partial(grad_kernel, size_gx, size_gy),
        grid_spec=pltpu.PrefetchScalarGridSpec(
            num_scalar_prefetch=1,
            grid=(blocks // GROUP,),
            in_specs=[pl.BlockSpec((GROUP, cells), lambda i, d: (i, 0))] * 2
            + [pl.BlockSpec((owners, rows, cols), lambda i, d: (0, 0, 0))],
            out_specs=pl.BlockSpec((2, GROUP, cells), lambda i, d: (0, i, 0)),
            scratch_shapes=[
                pltpu.VMEM((2, owners * rows, cols), jnp.float32),
                pltpu.VMEM((2, TROWS, GROUP, cols), jnp.float32),
            ],
        ),
        out_shape=jax.ShapeDtypeStruct((2, blocks, cells), jnp.float32),
        compiler_params=pltpu.CompilerParams(vmem_limit_bytes=VMEM_LIMIT),
        name="cell_grads",
    )(dest, cell_power, cell_bin, sens)


def roll(x, distance, axis):
    return pltpu.roll(x, distance % x.shape[axis], axis)


def remote(src, dst, sems, at, device):
    return pltpu.make_async_remote_copy(
        src_ref=src,
        dst_ref=dst,
        send_sem=sems.at[(0, *at)],
        recv_sem=sems.at[(1, *at)],
        device_id=device,
        device_id_type=pl.DeviceIdType.MESH,
    )


def sweep_kernel(
    size_gx,
    size_gy,
    mask_ref,
    temp_ref,
    cond_x_ref,
    cond_y_ref,
    cond_z_ref,
    weight_ref,
    partial_ref,
    temp_out,
    sens_out,
    west_s,
    south_s,
    inv_s,
    a_s,
    b_s,
    core_buf,
    x_buf,
    x_sum,
    y_buf,
    wide,
    sides,
    power_s,
    sens,
    stack_ref,
    row_bufs,
    packed,
    got,
    row_sems,
    col_sems,
    core_sems,
    x_sems,
    y_sems,
    halo_sems,
    back_y,
    back_x,
    back_core,
):
    layers = temp_ref.shape[0]
    _, rows, cols = partial_ref.shape
    size_x = size_gx // 2
    gx, gy = lax.axis_index("gx"), lax.axis_index("gy")
    x, core = gx // 2, lax.rem(gx, 2)
    partner = (x * 2 + 1 - core, gy)

    def ahead(dj):
        return lax.rem(gy + dj, size_gy)

    def behind(dj):
        return lax.rem(gy + size_gy - dj, size_gy)

    def x_ahead(d):
        return lax.rem(x + d, size_x)

    def x_behind(d):
        return lax.rem(x + size_x - d, size_x)

    barrier = pltpu.get_barrier_semaphore()
    for d in range(1, size_gx):
        pl.semaphore_signal(
            barrier,
            inc=1,
            device_id=(lax.rem(gx + d, size_gx), gy),
            device_id_type=pl.DeviceIdType.MESH,
        )
    for d in range(1, size_gy):
        pl.semaphore_signal(
            barrier, inc=1, device_id=(gx, ahead(d)), device_id_type=pl.DeviceIdType.MESH
        )
    pl.semaphore_wait(barrier, size_gx + size_gy - 2)

    def to_core(dj, t):
        src = partial_ref.at[(t * 2 + 1 - core) * size_gy + ahead(dj)]
        return remote(src, core_buf.at[t, dj], core_sems, (t, dj), partner)

    def to_x(dj, d):
        src = core_buf.at[x_ahead(d), dj]
        return remote(src, x_buf.at[d - 1, dj], x_sems, (d - 1, dj), (x_ahead(d) * 2 + core, gy))

    def to_y(dj):
        return remote(x_sum.at[dj], y_buf.at[dj - 1], y_sems, (dj - 1,), (gx, ahead(dj)))

    def chunk(k):
        return lax.rem(k + 1, size_gy)

    def loop(count, body, start=0):
        def wrapped(k, carry):
            body(k)
            return carry

        lax.fori_loop(start, count, wrapped, 0)

    def send_core(k):
        for t in range(size_x):
            to_core(chunk(k), t).start()

    args = (temp_ref, cond_x_ref, cond_y_ref, cond_z_ref, weight_ref)
    up, down = lax.rem(gx + 1, size_gx), lax.rem(gx + size_gx - 1, size_gx)
    arg_rows = []
    for k, ref in enumerate(args):
        arg_rows.append(
            remote(ref.at[:, pl.ds(rows - 8, 8)], row_bufs.at[0, k], row_sems, (0, k), (up, gy))
        )
        arg_rows.append(remote(ref.at[:, pl.ds(0, 8)], row_bufs.at[1, k], row_sems, (1, k), (down, gy)))
    for copy in arg_rows:
        copy.start()
    loop(size_gy, send_core)
    for k, ref in enumerate(args):
        for l in range(layers):
            stack_ref[k, l, :rows, :cols] = ref[l]
    for copy in arg_rows:
        copy.wait()
    for k in range(len(args)):
        for l in range(layers):
            stack_ref[k, l, rows : rows + 8, :cols] = jnp.where(gx < size_gx - 1, row_bufs[1, k, l], 0.0)
            stack_ref[k, l, rows + 8 :, :cols] = jnp.where(gx > 0, row_bufs[0, k, l], 0.0)
    slots = cols // SLOT
    slot_id = lax.broadcasted_iota(jnp.int32, wide.shape, 1) // SLOT
    for q in range(packed.shape[1]):
        to_left = jnp.zeros(wide.shape, jnp.float32)
        to_right = jnp.zeros(wide.shape, jnp.float32)
        for m in range(slots):
            k, l = divmod(q * slots + m, layers)
            if k < len(args):
                turned = roll(stack_ref[k, l, :, :cols], SLOT * m, 1)
                to_left = jnp.where(slot_id == m, turned, to_left)
                to_right = jnp.where(slot_id == (m - 1) % slots, turned, to_right)
        packed[0, q] = to_right
        packed[1, q] = to_left
    arg_cols = (
        remote(packed.at[0], got.at[0], col_sems, (0,), (gx, ahead(1))),
        remote(packed.at[1], got.at[1], col_sems, (1,), (gx, behind(1))),
    )
    for copy in arg_cols:
        copy.start()

    def send_x(k):
        dj = chunk(k)
        for t in range(size_x):
            to_core(dj, t).wait_recv()
            core_buf[t, dj] += partial_ref[(t * 2 + core) * size_gy + ahead(dj)]
        for d in range(1, size_x):
            to_x(dj, d).start()

    loop(size_gy, send_x)

    def add_x(dj):
        total = core_buf[x, dj]
        for d in range(1, size_x):
            to_x(dj, d).wait_recv()
            total = total + x_buf[d - 1, dj]
        x_sum[dj] = total

    def send_y(dj):
        add_x(dj)
        to_y(dj).start()

    loop(size_gy, send_y, 1)
    add_x(0)
    for copy in arg_cols:
        copy.wait()
    for q in range(packed.shape[1]):
        from_left = jnp.where(gy > 0, got[0, q], 0.0)
        from_right = jnp.where(gy < size_gy - 1, got[1, q], 0.0)
        for m in range(slots):
            k, l = divmod(q * slots + m, layers)
            if k < len(args):
                both = jnp.where(slot_id == m, from_right, 0.0)
                both = jnp.where(slot_id == (m - 1) % slots, from_left, both)
                stack_ref[k, l, :, cols:] = roll(both, -SLOT * m, 1)

    mask = mask_ref[...]
    for l in range(layers):
        east = stack_ref[1, l]
        north = stack_ref[2, l]
        west = roll(east, 1, 0)
        south = roll(north, 1, 1)
        diag = east + west + north + south + stack_ref[3, l]
        if l:
            diag = diag + stack_ref[3, l - 1]
        west_s[l] = west
        south_s[l] = south
        inv_s[l] = jnp.where(mask > 0.0, 1.0 / diag, 0.0)

    wide[:rows] = x_sum[0]

    def add_y(dj):
        to_y(dj).wait_recv()
        wide[:rows] += y_buf[dj - 1]

    loop(size_gy, add_y, 1)

    halo_rows = (
        remote(wide.at[pl.ds(rows - 8, 8)], wide.at[pl.ds(rows + 8, 8)], halo_sems, (0,), (up, gy)),
        remote(wide.at[pl.ds(0, 8)], wide.at[pl.ds(rows, 8)], halo_sems, (1,), (down, gy)),
    )
    for copy in halo_rows:
        copy.start()
    for copy in halo_rows:
        copy.wait()
    halo_cols = (
        remote(wide, sides.at[0], halo_sems, (2,), (gx, ahead(1))),
        remote(wide, sides.at[1], halo_sems, (3,), (gx, behind(1))),
    )
    for copy in halo_cols:
        copy.start()
    for copy in halo_cols:
        copy.wait()
    lane = lax.broadcasted_iota(jnp.int32, wide.shape, 1)
    power_s[:, :cols] = wide[...]
    power_s[:, cols:] = jnp.where(lane < cols // 2, sides[1], sides[0])

    def coupling(field, l):
        v = field(l)
        out = (
            stack_ref[1, l] * roll(v, -1, 0)
            + west_s[l] * roll(v, 1, 0)
            + stack_ref[2, l] * roll(v, -1, 1)
            + south_s[l] * roll(v, 1, 1)
        )
        if l + 1 < layers:
            out = out + stack_ref[3, l] * field(l + 1)
        if l:
            out = out + stack_ref[3, l - 1] * field(l - 1)
        return out

    def sweep(field, out_ref):
        for l in range(layers):
            summed = coupling(field, l)
            if l == 0:
                summed = summed + power_s[...]
            out_ref[l] = summed * inv_s[l]

    sweep(lambda l: stack_ref[0, l], a_s)
    sweep(lambda l: a_s[l], b_s)
    sweep(lambda l: b_s[l], a_s)
    for l in range(layers):
        temp_out[l] = a_s[l, :rows, :cols]
        b_s[l] = stack_ref[4, l] * a_s[l] * inv_s[l]
    for l in range(2):
        a_s[l] = coupling(lambda k: b_s[k], l) * inv_s[l]
    last = coupling(lambda k: a_s[k], 0) * inv_s[0]
    total = b_s[0] + a_s[0] + last
    sens[gx * size_gy + gy] = total[:rows, :cols]

    def give_y(dj):
        mine = sens.at[gx * size_gy + gy]
        return remote(mine, mine, back_y, (dj - 1,), (gx, ahead(dj)))

    def give_x(dj, d):
        block = sens.at[gx * size_gy + behind(dj)]
        return remote(block, block, back_x, (d - 1, dj), (x_ahead(d) * 2 + core, gy))

    def give_core(dj, d):
        block = sens.at[(x_behind(d) * 2 + core) * size_gy + behind(dj)]
        return remote(block, block, back_core, (d, dj), partner)

    def pass_on(dj):
        for d in range(1, size_x):
            give_x(dj, d).start()
        give_core(dj, 0).start()

    def receive_y(dj):
        give_y(dj).wait_recv()
        pass_on(dj)

    def receive_x(dj):
        for d in range(1, size_x):
            give_x(dj, d).wait_recv()
            give_core(dj, d).start()

    def finish(dj):
        for d in range(size_x):
            give_core(dj, d).wait_recv()
            give_core(dj, d).wait_send()
            to_core(dj, d).wait_send()
        for d in range(1, size_x):
            give_x(dj, d).wait_send()
            to_x(dj, d).wait_send()

    def finish_y(dj):
        give_y(dj).wait_send()
        to_y(dj).wait_send()

    loop(size_gy, lambda dj: give_y(dj).start(), 1)
    pass_on(0)
    loop(size_gy, receive_y, 1)
    loop(size_gy, receive_x)
    loop(size_gy, finish)
    loop(size_gy, finish_y, 1)

    def store(o):
        sens_out[o] = sens[o]

    loop(size_gx * size_gy, store)


def sweeps(mask, args, partial, size_gx, size_gy):
    owners, rows, cols = partial.shape
    layers = args[0].shape[0]
    wide_rows, wide_cols = mask.shape
    buffers = -(-len(args) * layers * SLOT // cols)
    size_x = size_gx // 2
    vmem = pl.BlockSpec(memory_space=pltpu.VMEM)

    def blocks(*lead, length=rows):
        return pltpu.VMEM((*lead, length, cols), jnp.float32)

    def sems(*shape):
        return pltpu.SemaphoreType.DMA((2, *shape))

    return pl.pallas_call(
        functools.partial(sweep_kernel, size_gx, size_gy),
        out_shape=(
            jax.ShapeDtypeStruct((layers, rows, cols), jnp.float32),
            jax.ShapeDtypeStruct((owners, rows, cols), jnp.float32),
        ),
        in_specs=[vmem] * (2 + len(args)),
        out_specs=(vmem, vmem),
        scratch_shapes=[pltpu.VMEM((layers, wide_rows, wide_cols), jnp.float32)] * 5
        + [
            blocks(size_x, size_gy),
            blocks(size_x - 1, size_gy),
            blocks(size_gy),
            blocks(size_gy - 1),
            blocks(length=wide_rows),
            blocks(2, length=wide_rows),
            pltpu.VMEM((wide_rows, wide_cols), jnp.float32),
            blocks(owners),
            pltpu.VMEM((len(args), layers, wide_rows, wide_cols), jnp.float32),
            blocks(2, len(args), layers, length=8),
            blocks(2, buffers, length=wide_rows),
            blocks(2, buffers, length=wide_rows),
            sems(2, len(args)),
            sems(2),
            sems(size_x, size_gy),
            sems(size_x - 1, size_gy),
            sems(size_gy - 1),
            sems(4),
            sems(size_gy - 1),
            sems(size_x - 1, size_gy),
            sems(size_x, size_gy),
        ],
        compiler_params=pltpu.CompilerParams(
            vmem_limit_bytes=56 * 1024 * 1024, collective_id=0, has_side_effects=True
        ),
        name="sweeps",
    )(mask, *args, partial)


def inside_mask(rows, cols):
    def axis_ok(axis, length, room):
        place = lax.broadcasted_iota(jnp.int32, (length + room,), 0)
        offset = jnp.where(place >= length + room // 2, place - (length + room), place)
        near = (offset >= -(HALO - 1)) & (offset < length + HALO - 1)
        whole = lax.axis_index(axis) * length + offset
        return near & (whole >= 0) & (whole < length * lax.axis_size(axis))

    ok = axis_ok("gx", rows, PAD_ROWS)[:, None] & axis_ok("gy", cols, cols)[None, :]
    return ok.astype(jnp.float32)


def on_device(
    cell_power, cell_bin, block_owner, block_tile, temp_prev, cond_x, cond_y, cond_z, weight
):
    _, rows, cols = temp_prev.shape
    tiles = rows // TROWS
    size_gx, size_gy = lax.axis_size("gx"), lax.axis_size("gy")
    devices = size_gx * size_gy
    dest = block_owner[:, 0] * tiles + block_tile
    args = (temp_prev, cond_x, cond_y, cond_z, weight)
    mask = inside_mask(rows, cols)
    partial = bin_cells(dest, cell_power, cell_bin, devices * rows, cols)
    partial = partial.reshape(devices, rows, cols)
    temperature, sens = sweeps(mask, args, partial, size_gx, size_gy)
    grads = cell_grads(dest, cell_power, cell_bin, sens, size_gx, size_gy)
    return temperature, grads


def solution(mesh):
    cells = P(("gx", "gy"), None)
    grid = P(None, "gx", "gy")
    return jax.shard_map(
        on_device,
        mesh=mesh,
        in_specs=(cells, cells, cells, P(("gx", "gy")), grid, grid, grid, grid, grid),
        out_specs=(grid, P(None, ("gx", "gy"), None)),
        check_vma=False,
    )
```

```python
import functools

import jax
import jax.numpy as jnp
from jax import lax
from jax.experimental import pallas as pl
from jax.experimental.pallas import tpu as pltpu
from jax.sharding import PartitionSpec as P

TROWS = 16
GROUP = 8
BATCH = 32
PARTS = 2
HALO = 5
PAD_ROWS = 16
SLOT = 8
VMEM_LIMIT = 48 * 1024 * 1024


def bin_kernel(dest_ref, power_ref, bin_ref, map_ref):
    step = pl.program_id(0)
    cells = power_ref.shape[1]
    cols = map_ref.shape[1]

    @pl.when(step == 0)
    def _():
        map_ref[...] = jnp.zeros_like(map_ref)

    for g in range(power_ref.shape[0] // GROUP):
        at = slice(g * GROUP, (g + 1) * GROUP)
        first = step * power_ref.shape[0] + g * GROUP
        power = power_ref[at, :]
        bins = bin_ref[at, :]
        high = power.astype(jnp.bfloat16)
        low = (power - high.astype(jnp.float32)).astype(jnp.bfloat16)
        narrow = cols // PARTS
        col = lax.bitwise_and(bins, narrow - 1)
        row = lax.shift_right_logical(bins, narrow.bit_length() - 1)
        col = col.astype(jnp.float32).astype(jnp.bfloat16)
        row = row.astype(jnp.float32).astype(jnp.bfloat16)
        col_iota = lax.broadcasted_iota(jnp.int32, (narrow, cells), 0).astype(jnp.float32).astype(jnp.bfloat16)
        line = lax.broadcasted_iota(jnp.int32, (TROWS * PARTS, cells), 0)
        line = lax.rem(line, TROWS) * PARTS + line // TROWS
        row_iota = line.astype(jnp.float32).astype(jnp.bfloat16)
        one = jnp.ones((), jnp.bfloat16)
        zero = jnp.zeros((), jnp.bfloat16)
        for s in range(GROUP):
            def spread(x, n):
                return jnp.broadcast_to(x[s : s + 1, :], (n, cells))

            col_hot = jnp.where(spread(col, narrow) == col_iota, one, zero)
            row_mask = spread(row, TROWS * PARTS) == row_iota
            left = jnp.concatenate(
                [
                    jnp.where(row_mask, spread(high, TROWS * PARTS), zero),
                    jnp.where(row_mask, spread(low, TROWS * PARTS), zero),
                ],
                axis=0,
            )
            tile = lax.dot_general(
                left, col_hot, (((1,), (1,)), ((), ())), preferred_element_type=jnp.float32
            )
            start = pl.multiple_of(dest_ref[first + s] * TROWS, TROWS)
            tile = tile[: TROWS * PARTS] + tile[TROWS * PARTS :]
            tile = [tile[p * TROWS : (p + 1) * TROWS] for p in range(PARTS)]
            map_ref[pl.ds(start, TROWS), :] += jnp.concatenate(tile, axis=1)


def bin_cells(dest, cell_power, cell_bin, map_rows, cols):
    blocks, cells = cell_power.shape
    return pl.pallas_call(
        bin_kernel,
        grid_spec=pltpu.PrefetchScalarGridSpec(
            num_scalar_prefetch=1,
            grid=(blocks // BATCH,),
            in_specs=[pl.BlockSpec((BATCH, cells), lambda i, d: (i, 0))] * 2,
            out_specs=pl.BlockSpec((map_rows, cols), lambda i, d: (0, 0)),
        ),
        out_shape=jax.ShapeDtypeStruct((map_rows, cols), jnp.float32),
        compiler_params=pltpu.CompilerParams(vmem_limit_bytes=VMEM_LIMIT),
        cost_estimate=pl.CostEstimate(
            flops=blocks * cells * cols * TROWS * 12, bytes_accessed=40 * 1024 * 1024, transcendentals=0
        ),
        name="bin_cells",
    )(dest, cell_power, cell_bin)


def grad_kernel(size_gx, size_gy, dest_ref, power_ref, bin_ref, sens_ref, out_ref, slope_ref, table_ref):
    step = pl.program_id(0)
    cells = power_ref.shape[1]
    owners, rows, cols = sens_ref.shape

    @pl.when(step == 0)
    def _():
        row_id = lax.broadcasted_iota(jnp.int32, (rows, cols), 0)
        col_id = lax.broadcasted_iota(jnp.int32, (rows, cols), 1)

        def one(o, carry):
            i = o // size_gy
            j = lax.rem(o, size_gy)
            here = sens_ref[o]
            above = sens_ref[jnp.maximum(o - size_gy, 0), rows - 1 :, :]
            below = sens_ref[jnp.minimum(o + size_gy, owners - 1), :1, :]
            above = jnp.where(i > 0, above, 0.0)
            below = jnp.where(i < size_gx - 1, below, 0.0)
            before = pltpu.roll(sens_ref[jnp.maximum(o - 1, 0)], 1, 1)
            after = pltpu.roll(sens_ref[jnp.minimum(o + 1, owners - 1)], cols - 1, 1)
            before = jnp.where(j > 0, before, 0.0)
            after = jnp.where(j < size_gy - 1, after, 0.0)
            down = jnp.where(row_id == rows - 1, below, pltpu.roll(here, rows - 1, 0))
            up = jnp.where(row_id == 0, above, pltpu.roll(here, 1, 0))
            right = jnp.where(col_id == cols - 1, after, pltpu.roll(here, cols - 1, 1))
            left = jnp.where(col_id == 0, before, pltpu.roll(here, 1, 1))
            at = pl.ds(pl.multiple_of(o * rows, rows), rows)
            slope_ref[0, at, :] = 0.5 * (down - up)
            slope_ref[1, at, :] = 0.5 * (right - left)
            return carry

        lax.fori_loop(0, owners, one, 0)

    for g in range(power_ref.shape[0] // GROUP):
        lines = slice(g * GROUP, (g + 1) * GROUP)
        first = step * power_ref.shape[0] + g * GROUP
        for s in range(GROUP):
            start = pl.multiple_of(dest_ref[first + s] * TROWS, TROWS)
            for a in range(2):
                table_ref[g, a, :, s, :] = slope_ref[a, pl.ds(start, TROWS), :]
        for c in range(cells // cols):
            at = slice(c * cols, (c + 1) * cols)
            bins = bin_ref[lines, at]
            power = power_ref[lines, at]
            col = lax.bitwise_and(bins, cols - 1)
            row = lax.shift_right_logical(bins, cols.bit_length() - 1)
            masks = [lax.bitwise_and(row, 1 << b) != 0 for b in range(4)]
            for a in range(2):
                picks = [
                    jnp.take_along_axis(table_ref[g, a, r], col, axis=1, mode="promise_in_bounds")
                    for r in range(TROWS)
                ]
                for mask in masks:
                    picks = [jnp.where(mask, picks[2 * k + 1], picks[2 * k]) for k in range(len(picks) // 2)]
                out_ref[a, lines, at] = picks[0] * power


def cell_grads(dest, cell_power, cell_bin, sens, size_gx, size_gy):
    blocks, cells = cell_power.shape
    owners, rows, cols = sens.shape
    return pl.pallas_call(
        functools.partial(grad_kernel, size_gx, size_gy),
        grid_spec=pltpu.PrefetchScalarGridSpec(
            num_scalar_prefetch=1,
            grid=(blocks // BATCH,),
            in_specs=[pl.BlockSpec((BATCH, cells), lambda i, d: (i, 0))] * 2
            + [pl.BlockSpec((owners, rows, cols), lambda i, d: (0, 0, 0))],
            out_specs=pl.BlockSpec((2, BATCH, cells), lambda i, d: (0, i, 0)),
            scratch_shapes=[
                pltpu.VMEM((2, owners * rows, cols), jnp.float32),
                pltpu.VMEM((BATCH // GROUP, 2, TROWS, GROUP, cols), jnp.float32),
            ],
        ),
        out_shape=jax.ShapeDtypeStruct((2, blocks, cells), jnp.float32),
        compiler_params=pltpu.CompilerParams(vmem_limit_bytes=VMEM_LIMIT),
        name="cell_grads",
    )(dest, cell_power, cell_bin, sens)


def roll(x, distance, axis):
    return pltpu.roll(x, distance % x.shape[axis], axis)


def remote(src, dst, sems, at, device):
    return pltpu.make_async_remote_copy(
        src_ref=src,
        dst_ref=dst,
        send_sem=sems.at[(0, *at)],
        recv_sem=sems.at[(1, *at)],
        device_id=device,
        device_id_type=pl.DeviceIdType.MESH,
    )


def sweep_kernel(
    size_gx,
    size_gy,
    mask_ref,
    temp_ref,
    cond_x_ref,
    cond_y_ref,
    cond_z_ref,
    weight_ref,
    partial_ref,
    temp_out,
    sens_out,
    west_s,
    south_s,
    inv_s,
    a_s,
    b_s,
    core_buf,
    x_buf,
    x_sum,
    y_buf,
    wide,
    sides,
    power_s,
    sens,
    stack_ref,
    row_bufs,
    packed,
    got,
    row_sems,
    col_sems,
    core_sems,
    x_sems,
    y_sems,
    halo_sems,
    back_y,
    back_x,
    back_core,
):
    layers = temp_ref.shape[0]
    _, rows, cols = partial_ref.shape
    size_x = size_gx // 2
    gx, gy = lax.axis_index("gx"), lax.axis_index("gy")
    x, core = gx // 2, lax.rem(gx, 2)
    partner = (x * 2 + 1 - core, gy)

    def ahead(dj):
        return lax.rem(gy + dj, size_gy)

    def behind(dj):
        return lax.rem(gy + size_gy - dj, size_gy)

    def x_ahead(d):
        return lax.rem(x + d, size_x)

    def x_behind(d):
        return lax.rem(x + size_x - d, size_x)

    barrier = pltpu.get_barrier_semaphore()
    for d in range(1, size_gx):
        pl.semaphore_signal(
            barrier,
            inc=1,
            device_id=(lax.rem(gx + d, size_gx), gy),
            device_id_type=pl.DeviceIdType.MESH,
        )
    for d in range(1, size_gy):
        pl.semaphore_signal(
            barrier, inc=1, device_id=(gx, ahead(d)), device_id_type=pl.DeviceIdType.MESH
        )
    pl.semaphore_wait(barrier, size_gx + size_gy - 2)

    def to_core(dj, t):
        src = partial_ref.at[(t * 2 + 1 - core) * size_gy + ahead(dj)]
        return remote(src, core_buf.at[t, dj], core_sems, (t, dj), partner)

    def to_x(dj, d):
        src = core_buf.at[x_ahead(d), dj]
        return remote(src, x_buf.at[d - 1, dj], x_sems, (d - 1, dj), (x_ahead(d) * 2 + core, gy))

    def to_y(dj):
        return remote(x_sum.at[dj], y_buf.at[dj - 1], y_sems, (dj - 1,), (gx, ahead(dj)))

    def chunk(k):
        return lax.rem(k + 1, size_gy)

    def loop(count, body, start=0):
        def wrapped(k, carry):
            body(k)
            return carry

        lax.fori_loop(start, count, wrapped, 0)

    def send_core(k):
        for t in range(size_x):
            to_core(chunk(k), t).start()

    args = (temp_ref, cond_x_ref, cond_y_ref, cond_z_ref, weight_ref)
    up, down = lax.rem(gx + 1, size_gx), lax.rem(gx + size_gx - 1, size_gx)
    arg_rows = []
    for k, ref in enumerate(args):
        arg_rows.append(
            remote(ref.at[:, pl.ds(rows - 8, 8)], row_bufs.at[0, k], row_sems, (0, k), (up, gy))
        )
        arg_rows.append(remote(ref.at[:, pl.ds(0, 8)], row_bufs.at[1, k], row_sems, (1, k), (down, gy)))
    for copy in arg_rows:
        copy.start()
    loop(size_gy, send_core)
    for k, ref in enumerate(args):
        for l in range(layers):
            stack_ref[k, l, :rows, :cols] = ref[l]
    for copy in arg_rows:
        copy.wait()
    for k in range(len(args)):
        for l in range(layers):
            stack_ref[k, l, rows : rows + 8, :cols] = jnp.where(gx < size_gx - 1, row_bufs[1, k, l], 0.0)
            stack_ref[k, l, rows + 8 :, :cols] = jnp.where(gx > 0, row_bufs[0, k, l], 0.0)
    slots = cols // SLOT
    slot_id = lax.broadcasted_iota(jnp.int32, wide.shape, 1) // SLOT
    for q in range(packed.shape[1]):
        to_left = jnp.zeros(wide.shape, jnp.float32)
        to_right = jnp.zeros(wide.shape, jnp.float32)
        for m in range(slots):
            k, l = divmod(q * slots + m, layers)
            if k < len(args):
                turned = roll(stack_ref[k, l, :, :cols], SLOT * m, 1)
                to_left = jnp.where(slot_id == m, turned, to_left)
                to_right = jnp.where(slot_id == (m - 1) % slots, turned, to_right)
        packed[0, q] = to_right
        packed[1, q] = to_left
    arg_cols = (
        remote(packed.at[0], got.at[0], col_sems, (0,), (gx, ahead(1))),
        remote(packed.at[1], got.at[1], col_sems, (1,), (gx, behind(1))),
    )
    for copy in arg_cols:
        copy.start()

    def send_x(k):
        dj = chunk(k)
        for t in range(size_x):
            to_core(dj, t).wait_recv()
            core_buf[t, dj] += partial_ref[(t * 2 + core) * size_gy + ahead(dj)]
        for d in range(1, size_x):
            to_x(dj, d).start()

    loop(size_gy, send_x)

    def add_x(dj):
        total = core_buf[x, dj]
        for d in range(1, size_x):
            to_x(dj, d).wait_recv()
            total = total + x_buf[d - 1, dj]
        x_sum[dj] = total

    def send_y(dj):
        add_x(dj)
        to_y(dj).start()

    loop(size_gy, send_y, 1)
    add_x(0)
    for copy in arg_cols:
        copy.wait()
    for q in range(packed.shape[1]):
        from_left = jnp.where(gy > 0, got[0, q], 0.0)
        from_right = jnp.where(gy < size_gy - 1, got[1, q], 0.0)
        for m in range(slots):
            k, l = divmod(q * slots + m, layers)
            if k < len(args):
                both = jnp.where(slot_id == m, from_right, 0.0)
                both = jnp.where(slot_id == (m - 1) % slots, from_left, both)
                stack_ref[k, l, :, cols:] = roll(both, -SLOT * m, 1)

    mask = mask_ref[...]
    for l in range(layers):
        east = stack_ref[1, l]
        north = stack_ref[2, l]
        west = roll(east, 1, 0)
        south = roll(north, 1, 1)
        diag = east + west + north + south + stack_ref[3, l]
        if l:
            diag = diag + stack_ref[3, l - 1]
        west_s[l] = west
        south_s[l] = south
        inv_s[l] = jnp.where(mask > 0.0, 1.0 / diag, 0.0)

    wide[:rows] = x_sum[0]

    def add_y(dj):
        to_y(dj).wait_recv()
        wide[:rows] += y_buf[dj - 1]

    loop(size_gy, add_y, 1)

    halo_rows = (
        remote(wide.at[pl.ds(rows - 8, 8)], wide.at[pl.ds(rows + 8, 8)], halo_sems, (0,), (up, gy)),
        remote(wide.at[pl.ds(0, 8)], wide.at[pl.ds(rows, 8)], halo_sems, (1,), (down, gy)),
    )
    for copy in halo_rows:
        copy.start()
    for copy in halo_rows:
        copy.wait()
    halo_cols = (
        remote(wide, sides.at[0], halo_sems, (2,), (gx, ahead(1))),
        remote(wide, sides.at[1], halo_sems, (3,), (gx, behind(1))),
    )
    for copy in halo_cols:
        copy.start()
    for copy in halo_cols:
        copy.wait()
    lane = lax.broadcasted_iota(jnp.int32, wide.shape, 1)
    power_s[:, :cols] = wide[...]
    power_s[:, cols:] = jnp.where(lane < cols // 2, sides[1], sides[0])

    def coupling(field, l):
        v = field(l)
        out = (
            stack_ref[1, l] * roll(v, -1, 0)
            + west_s[l] * roll(v, 1, 0)
            + stack_ref[2, l] * roll(v, -1, 1)
            + south_s[l] * roll(v, 1, 1)
        )
        if l + 1 < layers:
            out = out + stack_ref[3, l] * field(l + 1)
        if l:
            out = out + stack_ref[3, l - 1] * field(l - 1)
        return out

    def sweep(field, out_ref):
        for l in range(layers):
            summed = coupling(field, l)
            if l == 0:
                summed = summed + power_s[...]
            out_ref[l] = summed * inv_s[l]

    sweep(lambda l: stack_ref[0, l], a_s)
    sweep(lambda l: a_s[l], b_s)
    sweep(lambda l: b_s[l], a_s)
    for l in range(layers):
        temp_out[l] = a_s[l, :rows, :cols]
        b_s[l] = stack_ref[4, l] * a_s[l] * inv_s[l]
    for l in range(2):
        a_s[l] = coupling(lambda k: b_s[k], l) * inv_s[l]
    last = coupling(lambda k: a_s[k], 0) * inv_s[0]
    total = b_s[0] + a_s[0] + last
    sens[gx * size_gy + gy] = total[:rows, :cols]

    def give_y(dj):
        mine = sens.at[gx * size_gy + gy]
        return remote(mine, mine, back_y, (dj - 1,), (gx, ahead(dj)))

    def give_x(dj, d):
        block = sens.at[gx * size_gy + behind(dj)]
        return remote(block, block, back_x, (d - 1, dj), (x_ahead(d) * 2 + core, gy))

    def give_core(dj, d):
        block = sens.at[(x_behind(d) * 2 + core) * size_gy + behind(dj)]
        return remote(block, block, back_core, (d, dj), partner)

    def pass_on(dj):
        for d in range(1, size_x):
            give_x(dj, d).start()
        give_core(dj, 0).start()

    def receive_y(dj):
        give_y(dj).wait_recv()
        pass_on(dj)

    def receive_x(dj):
        for d in range(1, size_x):
            give_x(dj, d).wait_recv()
            give_core(dj, d).start()

    def finish(dj):
        for d in range(size_x):
            give_core(dj, d).wait_recv()
            give_core(dj, d).wait_send()
            to_core(dj, d).wait_send()
        for d in range(1, size_x):
            give_x(dj, d).wait_send()
            to_x(dj, d).wait_send()

    def finish_y(dj):
        give_y(dj).wait_send()
        to_y(dj).wait_send()

    loop(size_gy, lambda dj: give_y(dj).start(), 1)
    pass_on(0)
    loop(size_gy, receive_y, 1)
    loop(size_gy, receive_x)
    loop(size_gy, finish)
    loop(size_gy, finish_y, 1)

    def store(o):
        sens_out[o] = sens[o]

    loop(size_gx * size_gy, store)


def sweeps(mask, args, partial, size_gx, size_gy):
    owners, rows, cols = partial.shape
    layers = args[0].shape[0]
    wide_rows, wide_cols = mask.shape
    buffers = -(-len(args) * layers * SLOT // cols)
    size_x = size_gx // 2
    vmem = pl.BlockSpec(memory_space=pltpu.VMEM)

    def blocks(*lead, length=rows):
        return pltpu.VMEM((*lead, length, cols), jnp.float32)

    def sems(*shape):
        return pltpu.SemaphoreType.DMA((2, *shape))

    return pl.pallas_call(
        functools.partial(sweep_kernel, size_gx, size_gy),
        out_shape=(
            jax.ShapeDtypeStruct((layers, rows, cols), jnp.float32),
            jax.ShapeDtypeStruct((owners, rows, cols), jnp.float32),
        ),
        in_specs=[vmem] * (2 + len(args)),
        out_specs=(vmem, vmem),
        scratch_shapes=[pltpu.VMEM((layers, wide_rows, wide_cols), jnp.float32)] * 5
        + [
            blocks(size_x, size_gy),
            blocks(size_x - 1, size_gy),
            blocks(size_gy),
            blocks(size_gy - 1),
            blocks(length=wide_rows),
            blocks(2, length=wide_rows),
            pltpu.VMEM((wide_rows, wide_cols), jnp.float32),
            blocks(owners),
            pltpu.VMEM((len(args), layers, wide_rows, wide_cols), jnp.float32),
            blocks(2, len(args), layers, length=8),
            blocks(2, buffers, length=wide_rows),
            blocks(2, buffers, length=wide_rows),
            sems(2, len(args)),
            sems(2),
            sems(size_x, size_gy),
            sems(size_x - 1, size_gy),
            sems(size_gy - 1),
            sems(4),
            sems(size_gy - 1),
            sems(size_x - 1, size_gy),
            sems(size_x, size_gy),
        ],
        compiler_params=pltpu.CompilerParams(
            vmem_limit_bytes=56 * 1024 * 1024, collective_id=0, has_side_effects=True
        ),
        name="sweeps",
    )(mask, *args, partial)


def inside_mask(rows, cols):
    def axis_ok(axis, length, room):
        place = lax.broadcasted_iota(jnp.int32, (length + room,), 0)
        offset = jnp.where(place >= length + room // 2, place - (length + room), place)
        near = (offset >= -(HALO - 1)) & (offset < length + HALO - 1)
        whole = lax.axis_index(axis) * length + offset
        return near & (whole >= 0) & (whole < length * lax.axis_size(axis))

    ok = axis_ok("gx", rows, PAD_ROWS)[:, None] & axis_ok("gy", cols, cols)[None, :]
    return ok.astype(jnp.float32)


def on_device(
    cell_power, cell_bin, block_owner, block_tile, temp_prev, cond_x, cond_y, cond_z, weight
):
    _, rows, cols = temp_prev.shape
    tiles = rows // TROWS
    size_gx, size_gy = lax.axis_size("gx"), lax.axis_size("gy")
    devices = size_gx * size_gy
    dest = block_owner[:, 0] * tiles + block_tile
    args = (temp_prev, cond_x, cond_y, cond_z, weight)
    mask = inside_mask(rows, cols)
    partial = bin_cells(dest, cell_power, cell_bin, devices * rows, cols)
    partial = partial.reshape(devices, rows, cols)
    temperature, sens = sweeps(mask, args, partial, size_gx, size_gy)
    grads = cell_grads(dest, cell_power, cell_bin, sens, size_gx, size_gy)
    return temperature, grads


def solution(mesh):
    cells = P(("gx", "gy"), None)
    grid = P(None, "gx", "gy")
    return jax.shard_map(
        on_device,
        mesh=mesh,
        in_specs=(cells, cells, cells, P(("gx", "gy")), grid, grid, grid, grid, grid),
        out_specs=(grid, P(None, ("gx", "gy"), None)),
        check_vma=False,
    )
```
